128 devices in a mesh: red: 4 (over z), ten: 32 (over y, x, core).
Axes of the slice: x: 4, y: 4, z: 4, core: 2. Of those that a mesh axis runs over, the one named last changes fastest.
Arguments:
- amps: bfloat16 [1024, 32768], P('red', 'ten'), may hold values from -6 to 6
- ladder_ints: bfloat16 [256, 48, 128, 128], P('ten', 'red'), may hold values from -0.09375 to 0.09375
- cycle_ints: bfloat16 [256, 48, 128, 128], P('ten', 'red'), may hold values from -0.09375 to 0.09375
- sym_sizes: int32 [8], replicated, may hold values from 1 to 48, 256 in all
- occ_energy: float32 [1024], P('red'), may hold values from -2 to -0.5
- vir_energy: float32 [32768], P('ten'), may hold values from 0.5 to 2.5
Outputs:
- update: float32 [1024, 32768], P('red', 'ten')
The draws below stay inside these ranges and needn't reach their ends.
Inputs may be any that keep to these rules, and one draw needn't show every extreme that they name: sym_sizes sum to 256; the largest is exactly 48.
All inputs are finite; a program needn't handle non-finite values.
Results may differ from the reference program's by a relative error of at most 0.0029.
Values may be sent and summed in bfloat16 or wider, within the bound.
A program may use at most 320 MiB of HBM per device.

```python
import math
import jax
import jax.numpy as jnp
import numpy as np
from jax import lax

BS = 128
OCC_PAIRS = 1024
SLOTS = 48
NSYM = 8
NPB = 256


def level_of(own_key, extent, split, smallest, high):
    def one(position, parts):
        draws = jax.random.uniform(jax.random.fold_in(jax.random.fold_in(own_key, 6), position), (parts,), jnp.float32, smallest / len(split), high / len(split))
        return jnp.repeat(jnp.exp(draws), extent[position] // parts).reshape((-1,) + (1,) * (len(extent) - position - 1))

    factor_of = one(*split[0])
    for cut in split[1:]:
        factor_of = factor_of * one(*cut)
    return factor_of


def split_up(count, total, most, lean):
    loads = [(1 << 20) // math.isqrt(rank ** lean) + 1 for rank in range(2, count + 1)]
    surplus, holding = total - most - (count - 1), [1] * (count - 1)
    while surplus > 0:
        free = [i for i in range(count - 1) if holding[i] < most]
        mass, remaining = sum([loads[i] for i in free]), surplus
        for i in free:
            addition = min(most - holding[i], max(1, remaining * loads[i] // mass), surplus)
            holding[i] = holding[i] + addition
            surplus = surplus - addition
    return np.array([most] + holding)


def uneven(rng, count, total, bound, slope):
    if count == 2:
        one = jax.random.randint(rng, (), max(1, total - bound), min(bound, total - 1) + 1)
        return jnp.stack([one, total - one])
    tallies = jnp.asarray(split_up(count, total, bound, slope), jnp.int32)
    twos = (count - 1) // 2
    donor, receiver = tallies[1:1 + 2 * twos:2], tallies[2:2 + 2 * twos:2]
    room = jnp.minimum(donor - 1, bound - receiver)
    passed = jax.random.randint(jax.random.fold_in(rng, 1), (twos,), 0, 1 << 20) % (room + 1)
    tallies = tallies.at[1:1 + 2 * twos:2].set(donor - passed).at[2:2 + 2 * twos:2].set(receiver + passed)
    return tallies[jax.random.permutation(jax.random.fold_in(rng, 2), count)]


def noise(stream_key, shape, spread, most, cuts=(), kind=jnp.bfloat16):
    drawn = jax.random.normal(stream_key, shape, jnp.float32) * spread
    if len(cuts) > 0:
        drawn = level_of(stream_key, shape, cuts, -0.22, 0.18) * drawn
    return jnp.clip(drawn, min=-most, max=most).astype(kind)


def setup_inputs(seed: int = 0) -> dict:
    streams_of = jax.random.split(jax.random.key(seed), 7)
    return {
        "amps": noise(streams_of[0], (OCC_PAIRS, NPB * BS), 1.0, 6.0, ((0, 4), (1, 32))),
        "ladder_ints": noise(streams_of[1], (NPB, SLOTS, BS, BS), (NPB * BS // NSYM) ** -0.5, 0.09375, ((0, 32), (1, 4))),
        "cycle_ints": noise(streams_of[2], (NPB, SLOTS, BS, BS), (NPB * BS // NSYM) ** -0.5, 0.09375, ((0, 32), (1, 4))),
        "sym_sizes": uneven(streams_of[3], NSYM, NPB, SLOTS, 1).astype(jnp.int32),
        "occ_energy": jnp.clip(-2.0 + 1.5 * jax.random.uniform(streams_of[4], (OCC_PAIRS,), jnp.float32) ** level_of(streams_of[4], (OCC_PAIRS,), ((0, 4),), -0.2, 0.2), -2.0, -0.5),
        "vir_energy": jnp.clip(0.5 + 2.0 * jax.random.uniform(streams_of[5], (NPB * BS,), jnp.float32) ** level_of(streams_of[5], (NPB * BS,), ((0, 32),), -0.2, 0.2), 0.5, 2.5),
    }


def contract(operand, tiles, sym_sizes):
    npb = tiles.shape[0]
    slots = tiles.shape[1]
    width = tiles.shape[2]
    row_count = operand.shape[0]
    sym_ends = jnp.cumsum(sym_sizes).astype(jnp.int32)
    starts = (sym_ends - sym_sizes).astype(jnp.int32)
    padded = jnp.pad(operand.astype(jnp.float32), ((0, 0), (0, slots * width)))
    slot_index = (jnp.arange(slots * width, dtype=jnp.int32) // width).astype(jnp.int32)

    def one_block(block_at):
        member = (starts <= block_at) & (block_at < sym_ends)
        first_block = jnp.sum(jnp.where(member, starts, 0)).astype(jnp.int32)
        block_count = jnp.sum(jnp.where(member, sym_sizes, 0)).astype(jnp.int32)
        columns = lax.dynamic_slice_in_dim(padded, (first_block * width).astype(jnp.int32), slots * width, 1)
        slot_mask = (slot_index < block_count).astype(jnp.float32)
        tile_block = lax.dynamic_index_in_dim(tiles, block_at, 0, keepdims=False).astype(jnp.float32)
        return jnp.dot(columns * slot_mask[None, :], tile_block.reshape(slots * width, width), precision=lax.Precision.HIGHEST)

    blocks = lax.map(one_block, jnp.arange(npb, dtype=jnp.int32))
    return jnp.transpose(blocks, (1, 0, 2)).reshape(row_count, npb * width)


def reference(amps, ladder_ints, cycle_ints, sym_sizes, occ_energy, vir_energy):
    ladder = contract(amps, ladder_ints, sym_sizes)
    denom = vir_energy[None, :] - occ_energy[:, None]
    dressed = (amps.astype(jnp.float32) + ladder / denom).astype(jnp.bfloat16)
    cycle = contract(dressed, cycle_ints, sym_sizes)
    return dressed.astype(jnp.float32) + cycle / denom
```

```python
import functools

import jax
import jax.numpy as jnp
from jax import lax
from jax.experimental import pallas as pl
from jax.experimental.pallas import tpu as pltpu
from jax.sharding import PartitionSpec as P

MESH = pl.DeviceIdType.MESH
NZ = 4
NX = 4
BS = 128
SLOTS = 12
DEVB = 8
CHIPB = 2 * DEVB
DW = DEVB * BS
KW = SLOTS * BS
INNER = 14
WIN = 7 * CHIPB
HERE = 3 * CHIPB
CHUNKS = 2
ROWS = 128
M = ROWS // CHUNKS


def remote(src, dst, send, recv, device):
    return pltpu.make_async_remote_copy(
        src_ref=src,
        dst_ref=dst,
        send_sem=send,
        recv_sem=recv,
        device_id=device,
        device_id_type=MESH,
    )


def kernel(inner, sizes, amps, ints0, ints1, occ, vir, out, *scratch):
    scratch = list(scratch)

    def take(count):
        taken = scratch[:count]
        del scratch[:count]
        return taken

    win = [take(CHUNKS) for _ in range(2)]
    gathered = [take(CHUNKS) for _ in range(2)]
    packed = [take(CHUNKS) for _ in range(2)]
    packed_in = [take(CHUNKS) for _ in range(2)] if inner else None
    ints = take(2)
    part = take(CHUNKS)
    part_send = [take(CHUNKS) for _ in range(2)]
    part_recv = [take(CHUNKS) for _ in range(2)]
    (virs, stage, other_amps) = take(3)
    (x_s, x_r, y_s, y_r, z_s, z_r, zi_s, zi_r, p_s, p_r) = take(10)
    (w_s, w_r, w_l, a_s, a_r, v_s, v_r, o_s, o_r, o_l) = take(10)

    r = lax.axis_index("red")
    t = lax.axis_index("ten")
    h = lax.rem(t, 2)
    c = t // 2
    x = lax.rem(c, NX)
    y = c // NX

    def at(z, yy, xx, hh):
        return (z, (yy * NX + xx) * 2 + hh)

    sibling = at(r, y, x, 1 - h)

    def x_peer(d):
        return at(r, y, lax.rem(x + d, NX), h)

    def y_peer(d):
        return at(r, lax.rem(y + d + 4, 4), x, h)

    def z_to(d):
        return lax.rem(r + d, NZ)

    def z_peer(d):
        return at(z_to(d), y, x, h)

    peers = [sibling] + [x_peer(d) for d in (1, 2, 3)] + [y_peer(d) for d in (1, -1)]
    peers += [z_peer(d) for d in (1, 2, 3)]

    def group(block):
        start = jnp.int32(0)
        first, count = jnp.int32(0), jnp.int32(0)
        for g in range(8):
            size = sizes[g]
            inside = (start <= block) & (block < start + size)
            first = first + jnp.where(inside, start, 0)
            count = count + jnp.where(inside, size, 0)
            start = start + size
        return first, count

    head, head_n = group(c * CHIPB)
    tail, _ = group(c * CHIPB + CHIPB - 1)
    inner_at = jnp.minimum(head + head_n, (c + 1) * CHIPB)
    window_at = (c - 3) * CHIPB

    row0 = h * ROWS

    def sibling_amps(k):
        return remote(
            other_amps.at[k],
            win[0][k].at[pl.ds(HERE + h * DEVB, DEVB)],
            a_s.at[k],
            a_r.at[k],
            sibling,
        )

    def local_ints(p):
        return pltpu.make_async_copy(
            (ints0, ints1)[p], ints[p].at[pl.ds(h * DEVB, DEVB)], w_l.at[p]
        )

    def sibling_ints(p):
        return remote(
            (ints0, ints1)[p],
            ints[p].at[pl.ds(h * DEVB, DEVB)],
            w_s.at[p],
            w_r.at[p],
            sibling,
        )

    def sibling_vir():
        return remote(vir, virs.at[pl.ds(h * DEVB, DEVB)], v_s, v_r, sibling)

    def x_send(p, k, d):
        there = lax.rem(x + d, NX)
        return remote(
            win[p][k].at[pl.ds(HERE, CHIPB)],
            win[p][k].at[pl.ds((x - there + 3) * CHIPB, CHIPB)],
            x_s.at[p, k, d - 1],
            x_r.at[p, k, d - 1],
            x_peer(d),
        )

    def y_send(p, k, o):
        up = o > 0
        to = o - 4 if up else o + 4
        index = o + 3 if o < 0 else o + 2
        return remote(
            win[p][k].at[pl.ds((o + 3) * CHIPB, CHIPB)],
            win[p][k].at[pl.ds((to + 3) * CHIPB, CHIPB)],
            y_s.at[p, k, index],
            y_r.at[p, k, index],
            y_peer(1 if up else -1),
        )

    def y_each(p, k, act):
        for o in (-3, -2, -1, 1, 2, 3):
            has = (x + o <= 3) if o > 0 else (x + o >= 0)

            @pl.when(has)
            def _():
                act(y_send(p, k, o))

    def z_send(p, k, d):
        return remote(
            packed[p][k].at[d - 1],
            gathered[p][k].at[pl.ds(0, 2 * SLOTS), pl.ds(pl.multiple_of(r * M, M), M)],
            z_s.at[p, k, d - 1],
            z_r.at[p, k, d - 1],
            z_peer(d),
        )

    def zi_send(p, k, d):
        return remote(
            packed_in[p][k],
            gathered[p][k].at[
                pl.ds(2 * SLOTS, INNER), pl.ds(pl.multiple_of(r * M, M), M)
            ],
            zi_s.at[p, k, d - 1],
            zi_r.at[p, k, d - 1],
            z_peer(d),
        )

    def p_send(p, k, d):
        return remote(
            part_send[p][k].at[z_to(d)],
            part_recv[p][k].at[d - 1],
            p_s.at[p, k, d - 1],
            p_r.at[p, k, d - 1],
            z_peer(d),
        )

    def local_out(k):
        return pltpu.make_async_copy(
            stage.at[k, 0], out.at[pl.ds(row0 + k * M, M), :], o_l.at[k]
        )

    def sibling_out(k):
        return remote(
            stage.at[k, 1],
            out.at[pl.ds(row0 + k * M, M), :],
            o_s.at[k],
            o_r.at[k],
            sibling,
        )

    barrier = pltpu.get_barrier_semaphore()
    for peer in peers:
        pl.semaphore_signal(barrier, inc=1, device_id=peer, device_id_type=MESH)
    for p in range(2):
        local_ints(p).start()
    for k in range(CHUNKS):
        mine = pl.ds(pl.multiple_of(row0 + k * M, M), M)
        theirs = pl.ds(pl.multiple_of((1 - h) * ROWS + k * M, M), M)
        for b in range(DEVB):
            columns = slice(b * BS, (b + 1) * BS)
            win[0][k][HERE + h * DEVB + b] = amps[mine, columns]
            other_amps[k, b] = amps[theirs, columns]
    pl.semaphore_wait(barrier, len(peers))

    for k in range(CHUNKS):
        sibling_amps(k).start()
    sibling_vir().start()
    for p in range(2):
        sibling_ints(p).start()

    def spread_row(p, k):
        if p == 0:
            sibling_amps(k).wait_recv()
        for d in (1, 3, 2):
            x_send(p, k, d).start()

    def spread_rows(p, k):
        for d in (1, 2, 3):
            x_send(p, k, d).wait_recv()
        y_each(p, k, lambda copy: copy.start())

    def exchange(p, k):
        y_each(p, k, lambda copy: copy.wait_recv())
        source = win[p][k]

        def piece(first, plane):
            start = jnp.clip(first - window_at, 0, WIN - NZ * SLOTS)
            return source[pl.ds(start + plane * SLOTS, SLOTS)]

        for d in (1, 3, 2):
            packed[p][k][d - 1, 0:SLOTS] = piece(head, z_to(d))
            packed[p][k][d - 1, SLOTS : 2 * SLOTS] = piece(tail, z_to(d))
            z_send(p, k, d).start()
        rows = pl.ds(pl.multiple_of(r * M, M), M)
        if inner:
            between = source[pl.ds(jnp.clip(inner_at - window_at, 0, WIN - INNER), INNER)]
            packed_in[p][k][...] = between
            for d in (1, 2, 3):

                @pl.when(z_to(d) < 2)
                def _():
                    zi_send(p, k, d).start()

            gathered[p][k][2 * SLOTS : 2 * SLOTS + INNER, rows] = between
        gathered[p][k][0:SLOTS, rows] = piece(head, r)
        gathered[p][k][SLOTS : 2 * SLOTS, rows] = piece(tail, r)

    def multiply(p, k):
        for d in (1, 2, 3):
            z_send(p, k, d).wait_recv()
        if inner:

            @pl.when(r < 2)
            def _():
                for d in (1, 2, 3):
                    zi_send(p, k, d).wait_recv()

        @pl.loop(0, CHIPB)
        def _(q):
            first, count = group(c * CHIPB + q)
            base = jnp.where(first == head, 0, SLOTS)
            if inner:
                between = (first != head) & (first != tail)
                some = count > r * SLOTS
                place = 2 * SLOTS + first + r * SLOTS - inner_at
                base = jnp.where(between, jnp.where(some, place, 0), base)
                base = jnp.clip(base, 0, 2 * SLOTS + INNER - 1)
            tiles = gathered[p][k][pl.ds(base, SLOTS)]
            rows = jnp.concatenate([tiles[i] for i in range(SLOTS)], axis=1)
            product = jnp.dot(rows, ints[p][q], preferred_element_type=jnp.float32)
            product = product.reshape(NZ, M, BS)
            part[k][:, q] = product
            part_send[p][k][:, q] = product.astype(jnp.bfloat16)

        for d in (1, 3, 2):
            p_send(p, k, d).start()

    def finish(p, k):
        for d in (1, 2, 3):
            p_send(p, k, d).wait_recv()

        own = pl.ds(pl.multiple_of(row0 + k * M, M), M)

        @pl.loop(0, DEVB)
        def _(b):
            for side in range(2):
                q = (h if side == 0 else 1 - h) * DEVB + b
                total = part[k][r, q]
                for d in range(3):
                    total += part_recv[p][k][d, q].astype(jnp.float32)
                denom = virs[q] - occ[own, :]
                value = win[p][k][HERE + q].astype(jnp.float32) + total / denom
                if p == 0:
                    win[1][k][HERE + q] = value.astype(jnp.bfloat16)
                else:
                    stage[k, side, :, pl.ds(pl.multiple_of(b * BS, BS), BS)] = value

        if p == 1:
            sibling_out(k).start()
            local_out(k).start()

    def mask(p):
        local_ints(p).wait()
        sibling_ints(p).wait_recv()
        slot = lax.broadcasted_iota(jnp.int32, (KW, BS), 0)

        @pl.loop(0, CHIPB)
        def _(q):
            _, count = group(c * CHIPB + q)
            limit = (count - r * SLOTS) * BS
            tile = ints[p][q]
            ints[p][q] = jnp.where(slot < limit, tile, jnp.zeros_like(tile))

    for b in range(DEVB):
        virs[h * DEVB + b] = vir[b]
    if inner:
        for p in range(2):
            for k in range(CHUNKS):
                for b in range(2 * SLOTS + INNER, 3 * SLOTS + INNER - 1):
                    gathered[p][k][b] = jnp.zeros((NZ * M, BS), jnp.bfloat16)

    for k in range(CHUNKS):
        spread_row(0, k)
    for k in range(CHUNKS):
        spread_rows(0, k)
    for p in range(2):
        for k in range(CHUNKS):
            exchange(p, k)
        if p == 0:
            mask(0)
            mask(1)
            sibling_vir().wait_recv()
        for k in range(CHUNKS):
            multiply(p, k)
        for k in range(CHUNKS):
            finish(p, k)
            if p == 0:
                spread_row(1, k)
        if p == 0:
            for k in range(CHUNKS):
                spread_rows(1, k)

    for p in range(2):
        sibling_ints(p).wait_send()
        for k in range(CHUNKS):
            for d in (1, 2, 3):
                x_send(p, k, d).wait_send()
                z_send(p, k, d).wait_send()
                p_send(p, k, d).wait_send()
                if inner:

                    @pl.when(z_to(d) < 2)
                    def _():
                        zi_send(p, k, d).wait_send()

            y_each(p, k, lambda copy: copy.wait_send())
    sibling_vir().wait_send()
    for k in range(CHUNKS):
        sibling_amps(k).wait_send()
        local_out(k).wait()
        sibling_out(k).wait()


def call(inner, number, operands):
    bf16, f32 = jnp.bfloat16, jnp.float32
    width = 2 * SLOTS + (INNER + SLOTS - 1 if inner else 0)
    vmem = pltpu.VMEM
    dma = pltpu.SemaphoreType.DMA
    each = []
    each += [vmem((WIN, M, BS), bf16)] * (2 * CHUNKS)
    each += [vmem((width, NZ * M, BS), bf16)] * (2 * CHUNKS)
    each += [vmem((3, 2 * SLOTS, M, BS), bf16)] * (2 * CHUNKS)
    if inner:
        each += [vmem((INNER, M, BS), bf16)] * (2 * CHUNKS)
    each += [vmem((CHIPB, KW, BS), bf16)] * 2
    each += [vmem((NZ, CHIPB, M, BS), f32)] * CHUNKS
    each += [vmem((NZ, CHIPB, M, BS), bf16)] * (2 * CHUNKS)
    each += [vmem((3, CHIPB, M, BS), bf16)] * (2 * CHUNKS)
    each += [vmem((CHIPB, 1, BS), f32), vmem((CHUNKS, 2, M, DW), f32)]
    each += [vmem((CHUNKS, DEVB, M, BS), bf16)]
    three, six = (2, CHUNKS, 3), (2, CHUNKS, 6)
    each += [dma(s) for s in (three, three, six, six, three, three, three, three, three, three)]
    each += [dma((2,))] * 3 + [dma((CHUNKS,))] * 2 + [dma(())] * 2 + [dma((CHUNKS,))] * 3
    hbm = pl.BlockSpec(memory_space=pl.ANY)
    return pl.pallas_call(
        functools.partial(kernel, inner),
        name="ladders",
        out_shape=jax.ShapeDtypeStruct((2 * ROWS, DW), f32),
        in_specs=[
            pl.BlockSpec(memory_space=pltpu.SMEM),
            pl.BlockSpec(memory_space=pltpu.VMEM),
            hbm,
            hbm,
            pl.BlockSpec(memory_space=pltpu.VMEM),
            pl.BlockSpec(memory_space=pltpu.VMEM),
        ],
        out_specs=hbm,
        scratch_shapes=each,
        compiler_params=pltpu.CompilerParams(
            collective_id=number, has_side_effects=True, vmem_limit_bytes=60 << 20
        ),
    )(*operands)


def shards(amps, ladder_ints, cycle_ints, sym_sizes, occ_energy, vir_energy):
    operands = (
        sym_sizes,
        amps,
        ladder_ints.reshape(DEVB, KW, BS),
        cycle_ints.reshape(DEVB, KW, BS),
        occ_energy[:, None],
        vir_energy.reshape(DEVB, 1, BS),
    )
    return call(True, 1, operands)


def solution(mesh):
    placed = (
        P("red", "ten"),
        P("ten", "red", None, None),
        P("ten", "red", None, None),
        P(),
        P("red"),
        P("ten"),
    )
    return jax.shard_map(
        shards, mesh=mesh, in_specs=placed, out_specs=P("red", "ten"), check_vma=False
    )
```

```python
import functools

import jax
import jax.numpy as jnp
from jax import lax
from jax.experimental import pallas as pl
from jax.experimental.pallas import tpu as pltpu
from jax.sharding import PartitionSpec as P

MESH = pl.DeviceIdType.MESH
NZ = 4
NX = 4
BS = 128
SLOTS = 12
DEVB = 8
CHIPB = 2 * DEVB
DW = DEVB * BS
KW = SLOTS * BS
INNER = 14
WIN = 7 * CHIPB
HERE = 3 * CHIPB
CHUNKS = 8
ORDER = tuple(
    (tick - k // 2, k)
    for tick in range(10 + CHUNKS // 2 - 1)
    for k in reversed(range(CHUNKS))
    if 0 < tick - k // 2 < 10
)
ORDER = tuple((0, k) for k in range(CHUNKS)) + ORDER
ROWS = 128
M = ROWS // CHUNKS


def remote(src, dst, send, recv, device):
    return pltpu.make_async_remote_copy(
        src_ref=src,
        dst_ref=dst,
        send_sem=send,
        recv_sem=recv,
        device_id=device,
        device_id_type=MESH,
    )


def kernel(inner, sizes, amps, ints0, ints1, occ, vir, out, *scratch):
    scratch = list(scratch)

    def take(count):
        taken = scratch[:count]
        del scratch[:count]
        return taken

    win = [take(CHUNKS) for _ in range(2)]
    gathered = [take(CHUNKS) for _ in range(2)]
    packed = [take(CHUNKS) for _ in range(2)]
    packed_in = [take(CHUNKS) for _ in range(2)] if inner else None
    ints = take(2)
    part = take(CHUNKS)
    part_send = [take(CHUNKS) for _ in range(2)]
    part_recv = [take(CHUNKS) for _ in range(2)]
    (virs, stage, other_amps) = take(3)
    (x_s, x_r, y_s, y_r, z_s, z_r, zi_s, zi_r, p_s, p_r) = take(10)
    (w_s, w_r, w_l, a_s, a_r, v_s, v_r, o_s, o_r, o_l) = take(10)

    r = lax.axis_index("red")
    t = lax.axis_index("ten")
    h = lax.rem(t, 2)
    c = t // 2
    x = lax.rem(c, NX)
    y = c // NX

    def at(z, yy, xx, hh):
        return (z, (yy * NX + xx) * 2 + hh)

    sibling = at(r, y, x, 1 - h)

    def x_peer(d):
        return at(r, y, lax.rem(x + d, NX), h)

    def y_peer(d):
        return at(r, lax.rem(y + d + 4, 4), x, h)

    def z_to(d):
        return lax.rem(r + d, NZ)

    def z_peer(d):
        return at(z_to(d), y, x, h)

    peers = [sibling] + [x_peer(d) for d in (1, 2, 3)] + [y_peer(d) for d in (1, -1)]
    peers += [z_peer(d) for d in (1, 2, 3)]

    def group(block):
        start = jnp.int32(0)
        first, count = jnp.int32(0), jnp.int32(0)
        for g in range(8):
            size = sizes[g]
            inside = (start <= block) & (block < start + size)
            first = first + jnp.where(inside, start, 0)
            count = count + jnp.where(inside, size, 0)
            start = start + size
        return first, count

    head, head_n = group(c * CHIPB)
    tail, _ = group(c * CHIPB + CHIPB - 1)
    inner_at = jnp.minimum(head + head_n, (c + 1) * CHIPB)
    window_at = (c - 3) * CHIPB

    row0 = h * ROWS

    def sibling_amps(k):
        return remote(
            other_amps.at[k],
            win[0][k].at[pl.ds(HERE + h * DEVB, DEVB)],
            a_s.at[k],
            a_r.at[k],
            sibling,
        )

    def local_ints(p):
        return pltpu.make_async_copy(
            (ints0, ints1)[p], ints[p].at[pl.ds(h * DEVB, DEVB)], w_l.at[p]
        )

    def sibling_ints(p):
        return remote(
            (ints0, ints1)[p],
            ints[p].at[pl.ds(h * DEVB, DEVB)],
            w_s.at[p],
            w_r.at[p],
            sibling,
        )

    def sibling_vir():
        return remote(vir, virs.at[pl.ds(h * DEVB, DEVB)], v_s, v_r, sibling)

    def x_send(p, k, d):
        there = lax.rem(x + d, NX)
        return remote(
            win[p][k].at[pl.ds(HERE, CHIPB)],
            win[p][k].at[pl.ds((x - there + 3) * CHIPB, CHIPB)],
            x_s.at[p, k, d - 1],
            x_r.at[p, k, d - 1],
            x_peer(d),
        )

    def y_send(p, k, o):
        up = o > 0
        to = o - 4 if up else o + 4
        index = o + 3 if o < 0 else o + 2
        return remote(
            win[p][k].at[pl.ds((o + 3) * CHIPB, CHIPB)],
            win[p][k].at[pl.ds((to + 3) * CHIPB, CHIPB)],
            y_s.at[p, k, index],
            y_r.at[p, k, index],
            y_peer(1 if up else -1),
        )

    def y_each(p, k, act):
        for o in (-3, -2, -1, 1, 2, 3):
            has = (x + o <= 3) if o > 0 else (x + o >= 0)

            @pl.when(has)
            def _():
                act(y_send(p, k, o))

    def z_send(p, k, d):
        return remote(
            packed[p][k].at[d - 1],
            gathered[p][k].at[pl.ds(0, 2 * SLOTS), pl.ds(pl.multiple_of(r * M, M), M)],
            z_s.at[p, k, d - 1],
            z_r.at[p, k, d - 1],
            z_peer(d),
        )

    def zi_send(p, k, d):
        return remote(
            packed_in[p][k],
            gathered[p][k].at[
                pl.ds(2 * SLOTS, INNER), pl.ds(pl.multiple_of(r * M, M), M)
            ],
            zi_s.at[p, k, d - 1],
            zi_r.at[p, k, d - 1],
            z_peer(d),
        )

    def p_send(p, k, d):
        return remote(
            part_send[p][k].at[z_to(d)],
            part_recv[p][k].at[d - 1],
            p_s.at[p, k, d - 1],
            p_r.at[p, k, d - 1],
            z_peer(d),
        )

    def local_out(k):
        return pltpu.make_async_copy(
            stage.at[k, 0], out.at[pl.ds(row0 + k * M, M), :], o_l.at[k]
        )

    def sibling_out(k):
        return remote(
            stage.at[k, 1],
            out.at[pl.ds(row0 + k * M, M), :],
            o_s.at[k],
            o_r.at[k],
            sibling,
        )

    barrier = pltpu.get_barrier_semaphore()
    for peer in peers:
        pl.semaphore_signal(barrier, inc=1, device_id=peer, device_id_type=MESH)
    for p in range(2):
        local_ints(p).start()
    for k in range(CHUNKS):
        mine = pl.ds(pl.multiple_of(row0 + k * M, M), M)
        theirs = pl.ds(pl.multiple_of((1 - h) * ROWS + k * M, M), M)
        for b in range(DEVB):
            columns = slice(b * BS, (b + 1) * BS)
            win[0][k][HERE + h * DEVB + b] = amps[mine, columns]
            other_amps[k, b] = amps[theirs, columns]
    pl.semaphore_wait(barrier, len(peers))

    for k in range(CHUNKS):
        sibling_amps(k).start()

    def spread_row(p, k):
        if p == 0:
            sibling_amps(k).wait_recv()
        for d in (1, 3, 2):
            x_send(p, k, d).start()

    def spread_rows(p, k):
        for d in (1, 2, 3):
            x_send(p, k, d).wait_recv()
        y_each(p, k, lambda copy: copy.start())

    def exchange(p, k):
        y_each(p, k, lambda copy: copy.wait_recv())
        source = win[p][k]

        def piece(first, plane):
            start = jnp.clip(first - window_at, 0, WIN - NZ * SLOTS)
            return source[pl.ds(start + plane * SLOTS, SLOTS)]

        for d in (1, 3, 2):
            packed[p][k][d - 1, 0:SLOTS] = piece(head, z_to(d))
            packed[p][k][d - 1, SLOTS : 2 * SLOTS] = piece(tail, z_to(d))
            z_send(p, k, d).start()
        rows = pl.ds(pl.multiple_of(r * M, M), M)
        if inner:
            between = source[pl.ds(jnp.clip(inner_at - window_at, 0, WIN - INNER), INNER)]
            packed_in[p][k][...] = between
            for d in (1, 2, 3):

                @pl.when(z_to(d) < 2)
                def _():
                    zi_send(p, k, d).start()

            gathered[p][k][2 * SLOTS : 2 * SLOTS + INNER, rows] = between
        gathered[p][k][0:SLOTS, rows] = piece(head, r)
        gathered[p][k][SLOTS : 2 * SLOTS, rows] = piece(tail, r)

    def multiply(p, k):
        for d in (1, 2, 3):
            z_send(p, k, d).wait_recv()
        if inner:

            @pl.when(r < 2)
            def _():
                for d in (1, 2, 3):
                    zi_send(p, k, d).wait_recv()

        @pl.loop(0, CHIPB)
        def _(q):
            first, count = group(c * CHIPB + q)
            base = jnp.where(first == head, 0, SLOTS)
            if inner:
                between = (first != head) & (first != tail)
                some = count > r * SLOTS
                place = 2 * SLOTS + first + r * SLOTS - inner_at
                base = jnp.where(between, jnp.where(some, place, 0), base)
                base = jnp.clip(base, 0, 2 * SLOTS + INNER - 1)
            tiles = gathered[p][k][pl.ds(base, SLOTS)]
            rows = jnp.concatenate([tiles[i] for i in range(SLOTS)], axis=1)
            product = jnp.dot(rows, ints[p][q], preferred_element_type=jnp.float32)
            product = product.reshape(NZ, M, BS)
            part[k][:, q] = product
            part_send[p][k][:, q] = product.astype(jnp.bfloat16)

        for d in (1, 3, 2):
            p_send(p, k, d).start()

    def finish(p, k):
        for d in (1, 2, 3):
            p_send(p, k, d).wait_recv()

        own = pl.ds(pl.multiple_of(row0 + k * M, M), M)

        @pl.loop(0, DEVB)
        def _(b):
            for side in range(2):
                q = (h if side == 0 else 1 - h) * DEVB + b
                total = part[k][r, q]
                for d in range(3):
                    total += part_recv[p][k][d, q].astype(jnp.float32)
                denom = virs[q] - occ[own, :]
                value = win[p][k][HERE + q].astype(jnp.float32) + total / denom
                if p == 0:
                    win[1][k][HERE + q] = value.astype(jnp.bfloat16)
                else:
                    stage[k, side, :, pl.ds(pl.multiple_of(b * BS, BS), BS)] = value

        if p == 1:
            sibling_out(k).start()
            local_out(k).start()

    def mask(p):
        local_ints(p).wait()
        sibling_ints(p).wait_recv()
        slot = lax.broadcasted_iota(jnp.int32, (KW, BS), 0)

        @pl.loop(0, CHIPB)
        def _(q):
            _, count = group(c * CHIPB + q)
            limit = (count - r * SLOTS) * BS
            tile = ints[p][q]
            ints[p][q] = jnp.where(slot < limit, tile, jnp.zeros_like(tile))

    for b in range(DEVB):
        virs[h * DEVB + b] = vir[b]
    if inner:
        for p in range(2):
            for k in range(CHUNKS):
                for b in range(2 * SLOTS + INNER, 3 * SLOTS + INNER - 1):
                    gathered[p][k][b] = jnp.zeros((NZ * M, BS), jnp.bfloat16)

    masked = set()
    steps = (spread_row, spread_rows, exchange, multiply, finish)

    def do(step, k):
        if step % 5 == 3 and step not in masked:
            masked.add(step)
            mask(step // 5)
            if step == 3:
                sibling_vir().wait_recv()
        steps[step % 5](step // 5, k)
        if step == 0 and k == CHUNKS - 1:
            sibling_vir().start()
            sibling_ints(0).start()
        if step == 2 and k == CHUNKS - 1:
            sibling_ints(1).start()

    for step, k in ORDER:
        do(step, k)

    for p in range(2):
        sibling_ints(p).wait_send()
        for k in range(CHUNKS):
            for d in (1, 2, 3):
                x_send(p, k, d).wait_send()
                z_send(p, k, d).wait_send()
                p_send(p, k, d).wait_send()
                if inner:

                    @pl.when(z_to(d) < 2)
                    def _():
                        zi_send(p, k, d).wait_send()

            y_each(p, k, lambda copy: copy.wait_send())
    sibling_vir().wait_send()
    for k in range(CHUNKS):
        sibling_amps(k).wait_send()
        local_out(k).wait()
        sibling_out(k).wait()


def call(inner, number, operands):
    bf16, f32 = jnp.bfloat16, jnp.float32
    width = 2 * SLOTS + (INNER + SLOTS - 1 if inner else 0)
    vmem = pltpu.VMEM
    dma = pltpu.SemaphoreType.DMA
    each = []
    each += [vmem((WIN, M, BS), bf16)] * (2 * CHUNKS)
    each += [vmem((width, NZ * M, BS), bf16)] * (2 * CHUNKS)
    each += [vmem((3, 2 * SLOTS, M, BS), bf16)] * (2 * CHUNKS)
    if inner:
        each += [vmem((INNER, M, BS), bf16)] * (2 * CHUNKS)
    each += [vmem((CHIPB, KW, BS), bf16)] * 2
    each += [vmem((NZ, CHIPB, M, BS), f32)] * CHUNKS
    each += [vmem((NZ, CHIPB, M, BS), bf16)] * (2 * CHUNKS)
    each += [vmem((3, CHIPB, M, BS), bf16)] * (2 * CHUNKS)
    each += [vmem((CHIPB, 1, BS), f32), vmem((CHUNKS, 2, M, DW), f32)]
    each += [vmem((CHUNKS, DEVB, M, BS), bf16)]
    three, six = (2, CHUNKS, 3), (2, CHUNKS, 6)
    each += [dma(s) for s in (three, three, six, six, three, three, three, three, three, three)]
    each += [dma((2,))] * 3 + [dma((CHUNKS,))] * 2 + [dma(())] * 2 + [dma((CHUNKS,))] * 3
    hbm = pl.BlockSpec(memory_space=pl.ANY)
    return pl.pallas_call(
        functools.partial(kernel, inner),
        name="ladders",
        out_shape=jax.ShapeDtypeStruct((2 * ROWS, DW), f32),
        in_specs=[
            pl.BlockSpec(memory_space=pltpu.SMEM),
            pl.BlockSpec(memory_space=pltpu.VMEM),
            hbm,
            hbm,
            pl.BlockSpec(memory_space=pltpu.VMEM),
            pl.BlockSpec(memory_space=pltpu.VMEM),
        ],
        out_specs=hbm,
        scratch_shapes=each,
        compiler_params=pltpu.CompilerParams(
            collective_id=number, has_side_effects=True, vmem_limit_bytes=60 << 20
        ),
    )(*operands)


def shards(amps, ladder_ints, cycle_ints, sym_sizes, occ_energy, vir_energy):
    operands = (
        sym_sizes,
        amps,
        ladder_ints.reshape(DEVB, KW, BS),
        cycle_ints.reshape(DEVB, KW, BS),
        occ_energy[:, None],
        vir_energy.reshape(DEVB, 1, BS),
    )
    index = jnp.arange(sym_sizes.shape[0])
    upto = index[None, :] <= index[:, None]
    ends = jnp.sum(jnp.where(upto, sym_sizes[None, :], 0), axis=1)
    starts = ends - sym_sizes
    inside = (starts // CHIPB == ends // CHIPB) & (starts % CHIPB != 0)
    return lax.cond(
        jnp.any(inside),
        functools.partial(call, True, 1),
        functools.partial(call, False, 2),
        operands,
    )


def solution(mesh):
    placed = (
        P("red", "ten"),
        P("ten", "red", None, None),
        P("ten", "red", None, None),
        P(),
        P("red"),
        P("ten"),
    )
    return jax.shard_map(
        shards, mesh=mesh, in_specs=placed, out_specs=P("red", "ten"), check_vma=False
    )
```

```python
import functools

import jax
import jax.numpy as jnp
from jax import lax
from jax.experimental import pallas as pl
from jax.experimental.pallas import tpu as pltpu
from jax.sharding import PartitionSpec as P

MESH = pl.DeviceIdType.MESH
NZ = 4
NX = 4
BS = 128
SLOTS = 12
DEVB = 8
CHIPB = 2 * DEVB
DW = DEVB * BS
KW = SLOTS * BS
LEVELS = ((0, 0), (5, 1), (12, 1), (14, 2))
WIN = 7 * CHIPB
HERE = 3 * CHIPB
CHUNKS = 8
ORDER = tuple(
    (tick - k // 2, k)
    for tick in range(10 + CHUNKS // 2 - 1)
    for k in reversed(range(CHUNKS))
    if 0 < tick - k // 2 < 10
)
ORDER = tuple((0, k) for k in range(CHUNKS)) + ORDER
ROWS = 128
M = ROWS // CHUNKS


def remote(src, dst, send, recv, device):
    return pltpu.make_async_remote_copy(
        src_ref=src,
        dst_ref=dst,
        send_sem=send,
        recv_sem=recv,
        device_id=device,
        device_id_type=MESH,
    )


def kernel(level, sizes, amps, ints0, ints1, occ, vir, out, *scratch):
    (inner, planes) = level
    scratch = list(scratch)

    def take(count):
        taken = scratch[:count]
        del scratch[:count]
        return taken

    win = [take(CHUNKS) for _ in range(2)]
    gathered = [take(CHUNKS) for _ in range(2)]
    packed = [take(CHUNKS) for _ in range(2)]
    packed_in = [take(CHUNKS) for _ in range(2)] if inner else None
    ints = take(2)
    part = take(CHUNKS)
    part_send = [take(CHUNKS) for _ in range(2)]
    part_recv = [take(CHUNKS) for _ in range(2)]
    (virs, stage, other_amps) = take(3)
    (x_s, x_r, y_s, y_r, z_s, z_r, zi_s, zi_r, p_s, p_r) = take(10)
    (w_s, w_r, w_l, a_s, a_r, v_s, v_r, o_s, o_r, o_l) = take(10)

    r = lax.axis_index("red")
    t = lax.axis_index("ten")
    h = lax.rem(t, 2)
    c = t // 2
    x = lax.rem(c, NX)
    y = c // NX

    def at(z, yy, xx, hh):
        return (z, (yy * NX + xx) * 2 + hh)

    sibling = at(r, y, x, 1 - h)

    def x_peer(d):
        return at(r, y, lax.rem(x + d, NX), h)

    def y_peer(d):
        return at(r, lax.rem(y + d + 4, 4), x, h)

    def z_to(d):
        return lax.rem(r + d, NZ)

    def z_peer(d):
        return at(z_to(d), y, x, h)

    peers = [sibling] + [x_peer(d) for d in (1, 2, 3)] + [y_peer(d) for d in (1, -1)]
    peers += [z_peer(d) for d in (1, 2, 3)]

    def group(block):
        start = jnp.int32(0)
        first, count = jnp.int32(0), jnp.int32(0)
        for g in range(8):
            size = sizes[g]
            inside = (start <= block) & (block < start + size)
            first = first + jnp.where(inside, start, 0)
            count = count + jnp.where(inside, size, 0)
            start = start + size
        return first, count

    head, head_n = group(c * CHIPB)
    tail, _ = group(c * CHIPB + CHIPB - 1)
    inner_at = jnp.minimum(head + head_n, (c + 1) * CHIPB)
    window_at = (c - 3) * CHIPB

    row0 = h * ROWS

    def sibling_amps(k):
        return remote(
            other_amps.at[k],
            win[0][k].at[pl.ds(HERE + h * DEVB, DEVB)],
            a_s.at[k],
            a_r.at[k],
            sibling,
        )

    def local_ints(p):
        return pltpu.make_async_copy(
            (ints0, ints1)[p], ints[p].at[pl.ds(h * DEVB, DEVB)], w_l.at[p]
        )

    def sibling_ints(p):
        return remote(
            (ints0, ints1)[p],
            ints[p].at[pl.ds(h * DEVB, DEVB)],
            w_s.at[p],
            w_r.at[p],
            sibling,
        )

    def sibling_vir():
        return remote(vir, virs.at[pl.ds(h * DEVB, DEVB)], v_s, v_r, sibling)

    def x_send(p, k, d):
        there = lax.rem(x + d, NX)
        return remote(
            win[p][k].at[pl.ds(HERE, CHIPB)],
            win[p][k].at[pl.ds((x - there + 3) * CHIPB, CHIPB)],
            x_s.at[p, k, d - 1],
            x_r.at[p, k, d - 1],
            x_peer(d),
        )

    def y_send(p, k, o):
        up = o > 0
        to = o - 4 if up else o + 4
        index = o + 3 if o < 0 else o + 2
        return remote(
            win[p][k].at[pl.ds((o + 3) * CHIPB, CHIPB)],
            win[p][k].at[pl.ds((to + 3) * CHIPB, CHIPB)],
            y_s.at[p, k, index],
            y_r.at[p, k, index],
            y_peer(1 if up else -1),
        )

    def y_each(p, k, act):
        for o in (-3, -2, -1, 1, 2, 3):
            has = (x + o <= 3) if o > 0 else (x + o >= 0)

            @pl.when(has)
            def _():
                act(y_send(p, k, o))

    def z_send(p, k, d):
        return remote(
            packed[p][k].at[d - 1],
            gathered[p][k].at[pl.ds(0, 2 * SLOTS), pl.ds(pl.multiple_of(r * M, M), M)],
            z_s.at[p, k, d - 1],
            z_r.at[p, k, d - 1],
            z_peer(d),
        )

    def zi_send(p, k, d):
        return remote(
            packed_in[p][k],
            gathered[p][k].at[
                pl.ds(2 * SLOTS, inner), pl.ds(pl.multiple_of(r * M, M), M)
            ],
            zi_s.at[p, k, d - 1],
            zi_r.at[p, k, d - 1],
            z_peer(d),
        )

    def p_send(p, k, d):
        return remote(
            part_send[p][k].at[z_to(d)],
            part_recv[p][k].at[d - 1],
            p_s.at[p, k, d - 1],
            p_r.at[p, k, d - 1],
            z_peer(d),
        )

    def local_out(k):
        return pltpu.make_async_copy(
            stage.at[k, 0], out.at[pl.ds(row0 + k * M, M), :], o_l.at[k]
        )

    def sibling_out(k):
        return remote(
            stage.at[k, 1],
            out.at[pl.ds(row0 + k * M, M), :],
            o_s.at[k],
            o_r.at[k],
            sibling,
        )

    barrier = pltpu.get_barrier_semaphore()
    for peer in peers:
        pl.semaphore_signal(barrier, inc=1, device_id=peer, device_id_type=MESH)
    for p in range(2):
        local_ints(p).start()
    for k in range(CHUNKS):
        mine = pl.ds(pl.multiple_of(row0 + k * M, M), M)
        theirs = pl.ds(pl.multiple_of((1 - h) * ROWS + k * M, M), M)
        for b in range(DEVB):
            columns = slice(b * BS, (b + 1) * BS)
            win[0][k][HERE + h * DEVB + b] = amps[mine, columns]
            other_amps[k, b] = amps[theirs, columns]
    pl.semaphore_wait(barrier, len(peers))

    for k in range(CHUNKS):
        sibling_amps(k).start()

    def spread_row(p, k):
        if p == 0:
            sibling_amps(k).wait_recv()
        for d in (1, 3, 2):
            x_send(p, k, d).start()

    def spread_rows(p, k):
        for d in (1, 2, 3):
            x_send(p, k, d).wait_recv()
        y_each(p, k, lambda copy: copy.start())

    def exchange(p, k):
        y_each(p, k, lambda copy: copy.wait_recv())
        source = win[p][k]

        def piece(first, plane):
            start = jnp.clip(first - window_at, 0, WIN - NZ * SLOTS)
            return source[pl.ds(start + plane * SLOTS, SLOTS)]

        for d in (1, 3, 2):
            packed[p][k][d - 1, 0:SLOTS] = piece(head, z_to(d))
            packed[p][k][d - 1, SLOTS : 2 * SLOTS] = piece(tail, z_to(d))
            z_send(p, k, d).start()
        rows = pl.ds(pl.multiple_of(r * M, M), M)
        if inner:
            between = source[pl.ds(jnp.clip(inner_at - window_at, 0, WIN - inner), inner)]
            packed_in[p][k][...] = between
            for d in (1, 2, 3):

                @pl.when(z_to(d) < planes)
                def _():
                    zi_send(p, k, d).start()

            gathered[p][k][2 * SLOTS : 2 * SLOTS + inner, rows] = between
        gathered[p][k][0:SLOTS, rows] = piece(head, r)
        gathered[p][k][SLOTS : 2 * SLOTS, rows] = piece(tail, r)

    def multiply(p, k):
        for d in (1, 2, 3):
            z_send(p, k, d).wait_recv()
        if inner:

            @pl.when(r < planes)
            def _():
                for d in (1, 2, 3):
                    zi_send(p, k, d).wait_recv()

        @pl.loop(0, CHIPB)
        def _(q):
            first, count = group(c * CHIPB + q)
            base = jnp.where(first == head, 0, SLOTS)
            if inner:
                between = (first != head) & (first != tail)
                some = count > r * SLOTS
                place = 2 * SLOTS + first + r * SLOTS - inner_at
                base = jnp.where(between, jnp.where(some, place, 0), base)
                base = jnp.clip(base, 0, 2 * SLOTS + inner - 1)
            tiles = gathered[p][k][pl.ds(base, SLOTS)]
            rows = jnp.concatenate([tiles[i] for i in range(SLOTS)], axis=1)
            product = jnp.dot(rows, ints[p][q], preferred_element_type=jnp.float32)
            product = product.reshape(NZ, M, BS)
            part[k][:, q] = product
            part_send[p][k][:, q] = product.astype(jnp.bfloat16)

        for d in (1, 3, 2):
            p_send(p, k, d).start()

    def finish(p, k):
        for d in (1, 2, 3):
            p_send(p, k, d).wait_recv()

        own = pl.ds(pl.multiple_of(row0 + k * M, M), M)

        @pl.loop(0, DEVB)
        def _(b):
            for side in range(2):
                q = (h if side == 0 else 1 - h) * DEVB + b
                total = part[k][r, q]
                for d in range(3):
                    total += part_recv[p][k][d, q].astype(jnp.float32)
                denom = virs[q] - occ[own, :]
                value = win[p][k][HERE + q].astype(jnp.float32) + total / denom
                if p == 0:
                    win[1][k][HERE + q] = value.astype(jnp.bfloat16)
                else:
                    stage[k, side, :, pl.ds(pl.multiple_of(b * BS, BS), BS)] = value

        if p == 1:
            sibling_out(k).start()
            local_out(k).start()

    def mask(p):
        local_ints(p).wait()
        sibling_ints(p).wait_recv()
        slot = lax.broadcasted_iota(jnp.int32, (KW, BS), 0)

        @pl.loop(0, CHIPB)
        def _(q):
            _, count = group(c * CHIPB + q)
            limit = (count - r * SLOTS) * BS
            tile = ints[p][q]
            ints[p][q] = jnp.where(slot < limit, tile, jnp.zeros_like(tile))

    for b in range(DEVB):
        virs[h * DEVB + b] = vir[b]
    if inner:
        for p in range(2):
            for k in range(CHUNKS):
                for b in range(2 * SLOTS + inner, 3 * SLOTS + inner - 1):
                    gathered[p][k][b] = jnp.zeros((NZ * M, BS), jnp.bfloat16)

    masked = set()
    steps = (spread_row, spread_rows, exchange, multiply, finish)

    def do(step, k):
        if step % 5 == 3 and step not in masked:
            masked.add(step)
            mask(step // 5)
            if step == 3:
                sibling_vir().wait_recv()
        steps[step % 5](step // 5, k)
        if step == 0 and k == CHUNKS - 1:
            sibling_vir().start()
            sibling_ints(0).start()
        if step == 2 and k == CHUNKS - 1:
            sibling_ints(1).start()

    for step, k in ORDER:
        do(step, k)

    for p in range(2):
        sibling_ints(p).wait_send()
        for k in range(CHUNKS):
            for d in (1, 2, 3):
                x_send(p, k, d).wait_send()
                z_send(p, k, d).wait_send()
                p_send(p, k, d).wait_send()
                if inner:

                    @pl.when(z_to(d) < planes)
                    def _():
                        zi_send(p, k, d).wait_send()

            y_each(p, k, lambda copy: copy.wait_send())
    sibling_vir().wait_send()
    for k in range(CHUNKS):
        sibling_amps(k).wait_send()
        local_out(k).wait()
        sibling_out(k).wait()


def call(number, operands):
    inner = LEVELS[number][0]
    bf16, f32 = jnp.bfloat16, jnp.float32
    width = 2 * SLOTS + (inner + SLOTS - 1 if inner else 0)
    vmem = pltpu.VMEM
    dma = pltpu.SemaphoreType.DMA
    each = []
    each += [vmem((WIN, M, BS), bf16)] * (2 * CHUNKS)
    each += [vmem((width, NZ * M, BS), bf16)] * (2 * CHUNKS)
    each += [vmem((3, 2 * SLOTS, M, BS), bf16)] * (2 * CHUNKS)
    if inner:
        each += [vmem((inner, M, BS), bf16)] * (2 * CHUNKS)
    each += [vmem((CHIPB, KW, BS), bf16)] * 2
    each += [vmem((NZ, CHIPB, M, BS), f32)] * CHUNKS
    each += [vmem((NZ, CHIPB, M, BS), bf16)] * (2 * CHUNKS)
    each += [vmem((3, CHIPB, M, BS), bf16)] * (2 * CHUNKS)
    each += [vmem((CHIPB, 1, BS), f32), vmem((CHUNKS, 2, M, DW), f32)]
    each += [vmem((CHUNKS, DEVB, M, BS), bf16)]
    three, six = (2, CHUNKS, 3), (2, CHUNKS, 6)
    each += [dma(s) for s in (three, three, six, six, three, three, three, three, three, three)]
    each += [dma((2,))] * 3 + [dma((CHUNKS,))] * 2 + [dma(())] * 2 + [dma((CHUNKS,))] * 3
    hbm = pl.BlockSpec(memory_space=pl.ANY)
    return pl.pallas_call(
        functools.partial(kernel, LEVELS[number]),
        name="ladders",
        out_shape=jax.ShapeDtypeStruct((2 * ROWS, DW), f32),
        in_specs=[
            pl.BlockSpec(memory_space=pltpu.SMEM),
            pl.BlockSpec(memory_space=pltpu.VMEM),
            hbm,
            hbm,
            pl.BlockSpec(memory_space=pltpu.VMEM),
            pl.BlockSpec(memory_space=pltpu.VMEM),
        ],
        out_specs=hbm,
        scratch_shapes=each,
        compiler_params=pltpu.CompilerParams(
            collective_id=1 + number, has_side_effects=True, vmem_limit_bytes=60 << 20
        ),
    )(*operands)


def shards(amps, ladder_ints, cycle_ints, sym_sizes, occ_energy, vir_energy):
    operands = (
        sym_sizes,
        amps,
        ladder_ints.reshape(DEVB, KW, BS),
        cycle_ints.reshape(DEVB, KW, BS),
        occ_energy[:, None],
        vir_energy.reshape(DEVB, 1, BS),
    )
    index = jnp.arange(sym_sizes.shape[0])
    upto = index[None, :] <= index[:, None]
    ends = jnp.sum(jnp.where(upto, sym_sizes[None, :], 0), axis=1)
    starts = ends - sym_sizes
    chip = starts // CHIPB
    inside = (chip == ends // CHIPB) & (starts % CHIPB != 0)
    together = inside[None, :] & (chip[None, :] == chip[:, None])
    most = jnp.max(jnp.sum(jnp.where(together, sym_sizes[None, :], 0), axis=1))
    level = sum((most > inner).astype(jnp.int32) for inner, _ in LEVELS[:-1])
    branches = [functools.partial(call, number) for number in range(len(LEVELS))]
    return lax.switch(level, branches, operands)


def solution(mesh):
    placed = (
        P("red", "ten"),
        P("ten", "red", None, None),
        P("ten", "red", None, None),
        P(),
        P("red"),
        P("ten"),
    )
    return jax.shard_map(
        shards, mesh=mesh, in_specs=placed, out_specs=P("red", "ten"), check_vma=False
    )
```

```python
import functools

import jax
import jax.numpy as jnp
from jax import lax
from jax.experimental import pallas as pl
from jax.experimental.pallas import tpu as pltpu
from jax.sharding import PartitionSpec as P

MESH = pl.DeviceIdType.MESH
NZ = 4
NX = 4
BS = 128
SLOTS = 12
DEVB = 8
CHIPB = 2 * DEVB
DW = DEVB * BS
KW = SLOTS * BS
LEVELS = ((0, 0), (5, 1), (12, 1), (14, 2))
WIN = 7 * CHIPB
HERE = 3 * CHIPB
CHUNKS = 8
TURNS = (
    0, 1, 2, 3, 4, 5, 6, 7, 0, 1, 2, 0, 3, 1, 4, 5, 2, 0, 6, 3, 1, 7, 4, 2,
    0, 5, 3, 6, 1, 7, 4, 2, 0, 0, 5, 3, 0, 6, 1, 1, 0, 7, 4, 1, 2, 2, 5, 3,
    3, 6, 2, 1, 0, 3, 7, 4, 4, 5, 5, 6, 6, 2, 1, 4, 3, 0, 7, 7, 5, 6, 2, 4,
    1, 7, 5, 3, 0, 2, 6, 4, 7, 1, 5, 3, 2, 6, 4, 7, 5, 3, 6, 4, 7, 5, 6, 7,
)
ORDER = tuple((TURNS[:i].count(k), k) for i, k in enumerate(TURNS))
ROWS = 128
M = ROWS // CHUNKS


def remote(src, dst, send, recv, device):
    return pltpu.make_async_remote_copy(
        src_ref=src,
        dst_ref=dst,
        send_sem=send,
        recv_sem=recv,
        device_id=device,
        device_id_type=MESH,
    )


def kernel(level, sizes, amps, ints0, ints1, occ, vir, out, *scratch):
    (inner, planes) = level
    scratch = list(scratch)

    def take(count):
        taken = scratch[:count]
        del scratch[:count]
        return taken

    win = [take(CHUNKS) for _ in range(2)]
    gathered = [take(CHUNKS) for _ in range(2)]
    packed = [take(CHUNKS) for _ in range(2)]
    packed_in = [take(CHUNKS) for _ in range(2)] if inner else None
    ints = take(2)
    part = take(CHUNKS)
    part_send = [take(CHUNKS) for _ in range(2)]
    part_recv = [take(CHUNKS) for _ in range(2)]
    (virs, stage, other_amps) = take(3)
    (x_s, x_r, y_s, y_r, z_s, z_r, zi_s, zi_r, p_s, p_r) = take(10)
    (w_s, w_r, w_l, a_s, a_r, v_s, v_r, o_s, o_r, o_l) = take(10)

    r = lax.axis_index("red")
    t = lax.axis_index("ten")
    h = lax.rem(t, 2)
    c = t // 2
    x = lax.rem(c, NX)
    y = c // NX

    def at(z, yy, xx, hh):
        return (z, (yy * NX + xx) * 2 + hh)

    sibling = at(r, y, x, 1 - h)

    def x_peer(d):
        return at(r, y, lax.rem(x + d, NX), h)

    def y_peer(d):
        return at(r, lax.rem(y + d + 4, 4), x, h)

    def z_to(d):
        return lax.rem(r + d, NZ)

    def z_peer(d):
        return at(z_to(d), y, x, h)

    peers = [sibling] + [x_peer(d) for d in (1, 2, 3)] + [y_peer(d) for d in (1, -1)]
    peers += [z_peer(d) for d in (1, 2, 3)]

    def group(block):
        start = jnp.int32(0)
        first, count = jnp.int32(0), jnp.int32(0)
        for g in range(8):
            size = sizes[g]
            inside = (start <= block) & (block < start + size)
            first = first + jnp.where(inside, start, 0)
            count = count + jnp.where(inside, size, 0)
            start = start + size
        return first, count

    head, head_n = group(c * CHIPB)
    tail, _ = group(c * CHIPB + CHIPB - 1)
    inner_at = jnp.minimum(head + head_n, (c + 1) * CHIPB)
    window_at = (c - 3) * CHIPB

    row0 = h * ROWS

    def sibling_amps(k):
        return remote(
            other_amps.at[k],
            win[0][k].at[pl.ds(HERE + h * DEVB, DEVB)],
            a_s.at[k],
            a_r.at[k],
            sibling,
        )

    def local_ints(p):
        return pltpu.make_async_copy(
            (ints0, ints1)[p], ints[p].at[pl.ds(h * DEVB, DEVB)], w_l.at[p]
        )

    def sibling_ints(p):
        return remote(
            (ints0, ints1)[p],
            ints[p].at[pl.ds(h * DEVB, DEVB)],
            w_s.at[p],
            w_r.at[p],
            sibling,
        )

    def sibling_vir():
        return remote(vir, virs.at[pl.ds(h * DEVB, DEVB)], v_s, v_r, sibling)

    def x_send(p, k, d):
        there = lax.rem(x + d, NX)
        return remote(
            win[p][k].at[pl.ds(HERE, CHIPB)],
            win[p][k].at[pl.ds((x - there + 3) * CHIPB, CHIPB)],
            x_s.at[p, k, d - 1],
            x_r.at[p, k, d - 1],
            x_peer(d),
        )

    def y_send(p, k, o):
        up = o > 0
        to = o - 4 if up else o + 4
        index = o + 3 if o < 0 else o + 2
        return remote(
            win[p][k].at[pl.ds((o + 3) * CHIPB, CHIPB)],
            win[p][k].at[pl.ds((to + 3) * CHIPB, CHIPB)],
            y_s.at[p, k, index],
            y_r.at[p, k, index],
            y_peer(1 if up else -1),
        )

    def y_each(p, k, act):
        for o in (-3, -2, -1, 1, 2, 3):
            has = (x + o <= 3) if o > 0 else (x + o >= 0)

            @pl.when(has)
            def _():
                act(y_send(p, k, o))

    def z_send(p, k, d):
        return remote(
            packed[p][k].at[d - 1],
            gathered[p][k].at[pl.ds(0, 2 * SLOTS), pl.ds(pl.multiple_of(r * M, M), M)],
            z_s.at[p, k, d - 1],
            z_r.at[p, k, d - 1],
            z_peer(d),
        )

    def zi_send(p, k, d):
        return remote(
            packed_in[p][k],
            gathered[p][k].at[
                pl.ds(2 * SLOTS, inner), pl.ds(pl.multiple_of(r * M, M), M)
            ],
            zi_s.at[p, k, d - 1],
            zi_r.at[p, k, d - 1],
            z_peer(d),
        )

    ways = ((2, 0, 2, 1), (2, 1, 2, 3), (1, 1, 0, 1), (3, 0, 0, 3), (1, 0, 1, 1), (3, 1, 1, 3))

    def p_send(p, k, way):
        (owner, half, kind, d) = ways[way]
        blocks = pl.ds(half * DEVB, DEVB)
        return remote(
            part_send[p][k].at[z_to(owner), blocks],
            part_recv[p][k].at[kind, blocks],
            p_s.at[p, k, way],
            p_r.at[p, k, way],
            z_peer(d),
        )

    def local_out(k):
        return pltpu.make_async_copy(
            stage.at[k, 0], out.at[pl.ds(row0 + k * M, M), :], o_l.at[k]
        )

    def sibling_out(k):
        return remote(
            stage.at[k, 1],
            out.at[pl.ds(row0 + k * M, M), :],
            o_s.at[k],
            o_r.at[k],
            sibling,
        )

    barrier = pltpu.get_barrier_semaphore()
    for peer in peers:
        pl.semaphore_signal(barrier, inc=1, device_id=peer, device_id_type=MESH)
    for p in range(2):
        local_ints(p).start()
    for k in range(CHUNKS):
        mine = pl.ds(pl.multiple_of(row0 + k * M, M), M)
        theirs = pl.ds(pl.multiple_of((1 - h) * ROWS + k * M, M), M)
        for b in range(DEVB):
            columns = slice(b * BS, (b + 1) * BS)
            win[0][k][HERE + h * DEVB + b] = amps[mine, columns]
            other_amps[k, b] = amps[theirs, columns]
    pl.semaphore_wait(barrier, len(peers))

    for k in range(CHUNKS):
        sibling_amps(k).start()

    def spread_row(p, k):
        if p == 0:
            sibling_amps(k).wait_recv()
        for d in (1, 3, 2):
            x_send(p, k, d).start()

    def spread_rows(p, k):
        for d in (1, 2, 3):
            x_send(p, k, d).wait_recv()
        y_each(p, k, lambda copy: copy.start())

    def exchange(p, k):
        y_each(p, k, lambda copy: copy.wait_recv())
        source = win[p][k]

        def piece(first, plane):
            start = jnp.clip(first - window_at, 0, WIN - NZ * SLOTS)
            return source[pl.ds(start + plane * SLOTS, SLOTS)]

        for d in (1, 3, 2):
            packed[p][k][d - 1, 0:SLOTS] = piece(head, z_to(d))
            packed[p][k][d - 1, SLOTS : 2 * SLOTS] = piece(tail, z_to(d))
            z_send(p, k, d).start()
        rows = pl.ds(pl.multiple_of(r * M, M), M)
        if inner:
            between = source[pl.ds(jnp.clip(inner_at - window_at, 0, WIN - inner), inner)]
            packed_in[p][k][...] = between
            for d in (1, 2, 3):

                @pl.when(z_to(d) < planes)
                def _():
                    zi_send(p, k, d).start()

            gathered[p][k][2 * SLOTS : 2 * SLOTS + inner, rows] = between
        gathered[p][k][0:SLOTS, rows] = piece(head, r)
        gathered[p][k][SLOTS : 2 * SLOTS, rows] = piece(tail, r)

    def multiply(p, k):
        for d in (1, 2, 3):
            z_send(p, k, d).wait_recv()
        if inner:

            @pl.when(r < planes)
            def _():
                for d in (1, 2, 3):
                    zi_send(p, k, d).wait_recv()

        @pl.loop(0, CHIPB)
        def _(q):
            first, count = group(c * CHIPB + q)
            base = jnp.where(first == head, 0, SLOTS)
            if inner:
                between = (first != head) & (first != tail)
                some = count > r * SLOTS
                place = 2 * SLOTS + first + r * SLOTS - inner_at
                base = jnp.where(between, jnp.where(some, place, 0), base)
                base = jnp.clip(base, 0, 2 * SLOTS + inner - 1)
            tiles = gathered[p][k][pl.ds(base, SLOTS)]
            rows = jnp.concatenate([tiles[i] for i in range(SLOTS)], axis=1)
            product = jnp.dot(rows, ints[p][q], preferred_element_type=jnp.float32)
            product = product.reshape(NZ, M, BS)
            part[k][:, q] = product
            part_send[p][k][:, q] = product.astype(jnp.bfloat16)

        for way in range(4):
            p_send(p, k, way).start()

    def relay(p, k):
        for half in range(2):
            p_send(p, k, half).wait_recv()
            blocks = slice(half * DEVB, (half + 1) * DEVB)
            owner = z_to((1, 3)[half])
            both = part[k][owner, blocks] + part_recv[p][k][2, blocks].astype(jnp.float32)
            part_send[p][k][owner, blocks] = both.astype(jnp.bfloat16)
            p_send(p, k, 4 + half).start()

    def finish(p, k):
        for way in range(2, 6):
            p_send(p, k, way).wait_recv()

        own = pl.ds(pl.multiple_of(row0 + k * M, M), M)

        @pl.loop(0, DEVB)
        def _(b):
            for side in range(2):
                q = (h if side == 0 else 1 - h) * DEVB + b
                total = part[k][r, q]
                for d in range(2):
                    total += part_recv[p][k][d, q].astype(jnp.float32)
                denom = virs[q] - occ[own, :]
                value = win[p][k][HERE + q].astype(jnp.float32) + total / denom
                if p == 0:
                    win[1][k][HERE + q] = value.astype(jnp.bfloat16)
                else:
                    stage[k, side, :, pl.ds(pl.multiple_of(b * BS, BS), BS)] = value

        if p == 1:
            sibling_out(k).start()
            local_out(k).start()

    def mask(p):
        local_ints(p).wait()
        sibling_ints(p).wait_recv()
        slot = lax.broadcasted_iota(jnp.int32, (KW, BS), 0)

        @pl.loop(0, CHIPB)
        def _(q):
            _, count = group(c * CHIPB + q)
            limit = (count - r * SLOTS) * BS
            tile = ints[p][q]
            ints[p][q] = jnp.where(slot < limit, tile, jnp.zeros_like(tile))

    for b in range(DEVB):
        virs[h * DEVB + b] = vir[b]
    if inner:
        for p in range(2):
            for k in range(CHUNKS):
                for b in range(2 * SLOTS + inner, 3 * SLOTS + inner - 1):
                    gathered[p][k][b] = jnp.zeros((NZ * M, BS), jnp.bfloat16)

    masked = set()
    steps = (spread_row, spread_rows, exchange, multiply, relay, finish)

    def do(step, k):
        if step % 6 == 3 and step not in masked:
            masked.add(step)
            mask(step // 6)
            if step == 3:
                sibling_vir().wait_recv()
        steps[step % 6](step // 6, k)
        if (step, k) == (0, 1):
            sibling_vir().start()
            sibling_ints(0).start()
        if (step, k) == (2, 1):
            sibling_ints(1).start()

    for step, k in ORDER:
        do(step, k)

    for p in range(2):
        sibling_ints(p).wait_send()
        for k in range(CHUNKS):
            for d in (1, 2, 3):
                x_send(p, k, d).wait_send()
                z_send(p, k, d).wait_send()
                if inner:

                    @pl.when(z_to(d) < planes)
                    def _():
                        zi_send(p, k, d).wait_send()

            for way in range(6):
                p_send(p, k, way).wait_send()
            y_each(p, k, lambda copy: copy.wait_send())
    sibling_vir().wait_send()
    for k in range(CHUNKS):
        sibling_amps(k).wait_send()
        local_out(k).wait()
        sibling_out(k).wait()


def call(number, operands):
    inner = LEVELS[number][0]
    bf16, f32 = jnp.bfloat16, jnp.float32
    width = 2 * SLOTS + (inner + SLOTS - 1 if inner else 0)
    vmem = pltpu.VMEM
    dma = pltpu.SemaphoreType.DMA
    each = []
    each += [vmem((WIN, M, BS), bf16)] * (2 * CHUNKS)
    each += [vmem((width, NZ * M, BS), bf16)] * (2 * CHUNKS)
    each += [vmem((3, 2 * SLOTS, M, BS), bf16)] * (2 * CHUNKS)
    if inner:
        each += [vmem((inner, M, BS), bf16)] * (2 * CHUNKS)
    each += [vmem((CHIPB, KW, BS), bf16)] * 2
    each += [vmem((NZ, CHIPB, M, BS), f32)] * CHUNKS
    each += [vmem((NZ, CHIPB, M, BS), bf16)] * (2 * CHUNKS)
    each += [vmem((3, CHIPB, M, BS), bf16)] * (2 * CHUNKS)
    each += [vmem((CHIPB, 1, BS), f32), vmem((CHUNKS, 2, M, DW), f32)]
    each += [vmem((CHUNKS, DEVB, M, BS), bf16)]
    three, six = (2, CHUNKS, 3), (2, CHUNKS, 6)
    each += [dma(s) for s in (three, three, six, six, three, three, three, three, six, six)]
    each += [dma((2,))] * 3 + [dma((CHUNKS,))] * 2 + [dma(())] * 2 + [dma((CHUNKS,))] * 3
    hbm = pl.BlockSpec(memory_space=pl.ANY)
    return pl.pallas_call(
        functools.partial(kernel, LEVELS[number]),
        name="ladders",
        out_shape=jax.ShapeDtypeStruct((2 * ROWS, DW), f32),
        in_specs=[
            pl.BlockSpec(memory_space=pltpu.SMEM),
            pl.BlockSpec(memory_space=pltpu.VMEM),
            hbm,
            hbm,
            pl.BlockSpec(memory_space=pltpu.VMEM),
            pl.BlockSpec(memory_space=pltpu.VMEM),
        ],
        out_specs=hbm,
        scratch_shapes=each,
        compiler_params=pltpu.CompilerParams(
            collective_id=1 + number, has_side_effects=True, vmem_limit_bytes=60 << 20
        ),
    )(*operands)


def shards(amps, ladder_ints, cycle_ints, sym_sizes, occ_energy, vir_energy):
    operands = (
        sym_sizes,
        amps,
        ladder_ints.reshape(DEVB, KW, BS),
        cycle_ints.reshape(DEVB, KW, BS),
        occ_energy[:, None],
        vir_energy.reshape(DEVB, 1, BS),
    )
    index = jnp.arange(sym_sizes.shape[0])
    upto = index[None, :] <= index[:, None]
    ends = jnp.sum(jnp.where(upto, sym_sizes[None, :], 0), axis=1)
    starts = ends - sym_sizes
    chip = starts // CHIPB
    inside = (chip == ends // CHIPB) & (starts % CHIPB != 0)
    together = inside[None, :] & (chip[None, :] == chip[:, None])
    most = jnp.max(jnp.sum(jnp.where(together, sym_sizes[None, :], 0), axis=1))
    level = sum((most > inner).astype(jnp.int32) for inner, _ in LEVELS[:-1])
    branches = [functools.partial(call, number) for number in range(len(LEVELS))]
    return lax.switch(level, branches, operands)


def solution(mesh):
    placed = (
        P("red", "ten"),
        P("ten", "red", None, None),
        P("ten", "red", None, None),
        P(),
        P("red"),
        P("ten"),
    )
    return jax.shard_map(
        shards, mesh=mesh, in_specs=placed, out_specs=P("red", "ten"), check_vma=False
    )
```

```python
import functools

import jax
import jax.numpy as jnp
from jax import lax
from jax.experimental import pallas as pl
from jax.experimental.pallas import tpu as pltpu
from jax.sharding import PartitionSpec as P

MESH = pl.DeviceIdType.MESH
NZ = 4
NX = 4
BS = 128
SLOTS = 12
DEVB = 8
CHIPB = 2 * DEVB
DW = DEVB * BS
KW = SLOTS * BS
LEVELS = ((0, 0), (4, 1), (8, 1), (12, 1), (14, 2))
WIN = 7 * CHIPB
HERE = 3 * CHIPB
CHUNKS = 8
TURNS = (
    0, 1, 2, 3, 4, 5, 6, 7, 0, 1, 2, 0, 3, 1, 4, 5, 2, 0, 6, 3, 1, 7, 4, 2,
    0, 5, 3, 6, 1, 7, 4, 2, 0, 0, 5, 3, 0, 6, 1, 1, 0, 7, 4, 1, 2, 2, 5, 3,
    3, 6, 2, 1, 0, 3, 7, 4, 4, 5, 5, 6, 6, 2, 1, 4, 3, 0, 7, 7, 5, 6, 2, 4,
    1, 7, 5, 3, 0, 2, 6, 4, 7, 1, 5, 3, 2, 6, 4, 7, 5, 3, 6, 4, 7, 5, 6, 7,
)
ORDER = tuple((TURNS[:i].count(k), k) for i, k in enumerate(TURNS))
ROWS = 128
M = ROWS // CHUNKS


def remote(src, dst, send, recv, device):
    return pltpu.make_async_remote_copy(
        src_ref=src,
        dst_ref=dst,
        send_sem=send,
        recv_sem=recv,
        device_id=device,
        device_id_type=MESH,
    )


def kernel(level, sizes, amps, ints0, ints1, occ, vir, out, *scratch):
    (inner, planes) = level
    scratch = list(scratch)

    def take(count):
        taken = scratch[:count]
        del scratch[:count]
        return taken

    win = [take(CHUNKS) for _ in range(2)]
    gathered = [take(CHUNKS) for _ in range(2)]
    packed = [take(CHUNKS) for _ in range(2)]
    packed_in = [take(CHUNKS) for _ in range(2)] if inner else None
    ints = take(2)
    part = take(CHUNKS)
    part_send = [take(CHUNKS) for _ in range(2)]
    part_recv = [take(CHUNKS) for _ in range(2)]
    (virs, stage, other_amps) = take(3)
    (x_s, x_r, y_s, y_r, z_s, z_r, zi_s, zi_r, p_s, p_r) = take(10)
    (w_s, w_r, w_l, a_s, a_r, v_s, v_r, o_s, o_r, o_l) = take(10)

    r = lax.axis_index("red")
    t = lax.axis_index("ten")
    h = lax.rem(t, 2)
    c = t // 2
    x = lax.rem(c, NX)
    y = c // NX

    def at(z, yy, xx, hh):
        return (z, (yy * NX + xx) * 2 + hh)

    sibling = at(r, y, x, 1 - h)

    def x_peer(d):
        return at(r, y, lax.rem(x + d, NX), h)

    def y_peer(d):
        return at(r, lax.rem(y + d + 4, 4), x, h)

    def z_to(d):
        return lax.rem(r + d, NZ)

    def z_peer(d):
        return at(z_to(d), y, x, h)

    peers = [sibling] + [x_peer(d) for d in (1, 2, 3)] + [y_peer(d) for d in (1, -1)]
    peers += [z_peer(d) for d in (1, 2, 3)]

    def group(block):
        start = jnp.int32(0)
        first, count = jnp.int32(0), jnp.int32(0)
        for g in range(8):
            size = sizes[g]
            inside = (start <= block) & (block < start + size)
            first = first + jnp.where(inside, start, 0)
            count = count + jnp.where(inside, size, 0)
            start = start + size
        return first, count

    head, head_n = group(c * CHIPB)
    tail, _ = group(c * CHIPB + CHIPB - 1)
    inner_at = jnp.minimum(head + head_n, (c + 1) * CHIPB)
    window_at = (c - 3) * CHIPB

    row0 = h * ROWS

    def sibling_amps(k):
        return remote(
            other_amps.at[k],
            win[0][k].at[pl.ds(HERE + h * DEVB, DEVB)],
            a_s.at[k],
            a_r.at[k],
            sibling,
        )

    def local_ints(p):
        return pltpu.make_async_copy(
            (ints0, ints1)[p], ints[p].at[pl.ds(h * DEVB, DEVB)], w_l.at[p]
        )

    def sibling_ints(p):
        return remote(
            (ints0, ints1)[p],
            ints[p].at[pl.ds(h * DEVB, DEVB)],
            w_s.at[p],
            w_r.at[p],
            sibling,
        )

    def sibling_vir():
        return remote(vir, virs.at[pl.ds(h * DEVB, DEVB)], v_s, v_r, sibling)

    def x_send(p, k, d):
        there = lax.rem(x + d, NX)
        return remote(
            win[p][k].at[pl.ds(HERE, CHIPB)],
            win[p][k].at[pl.ds((x - there + 3) * CHIPB, CHIPB)],
            x_s.at[p, k, d - 1],
            x_r.at[p, k, d - 1],
            x_peer(d),
        )

    def y_send(p, k, o):
        up = o > 0
        to = o - 4 if up else o + 4
        index = o + 3 if o < 0 else o + 2
        return remote(
            win[p][k].at[pl.ds((o + 3) * CHIPB, CHIPB)],
            win[p][k].at[pl.ds((to + 3) * CHIPB, CHIPB)],
            y_s.at[p, k, index],
            y_r.at[p, k, index],
            y_peer(1 if up else -1),
        )

    def y_each(p, k, act):
        for o in (-3, -2, -1, 1, 2, 3):
            has = (x + o <= 3) if o > 0 else (x + o >= 0)

            @pl.when(has)
            def _():
                act(y_send(p, k, o))

    def z_send(p, k, d):
        return remote(
            packed[p][k].at[d - 1],
            gathered[p][k].at[pl.ds(0, 2 * SLOTS), pl.ds(pl.multiple_of(r * M, M), M)],
            z_s.at[p, k, d - 1],
            z_r.at[p, k, d - 1],
            z_peer(d),
        )

    def zi_send(p, k, d):
        return remote(
            packed_in[p][k],
            gathered[p][k].at[
                pl.ds(2 * SLOTS, inner), pl.ds(pl.multiple_of(r * M, M), M)
            ],
            zi_s.at[p, k, d - 1],
            zi_r.at[p, k, d - 1],
            z_peer(d),
        )

    ways = ((2, 0, 2, 1), (2, 1, 2, 3), (1, 1, 0, 1), (3, 0, 0, 3), (1, 0, 1, 1), (3, 1, 1, 3))

    def p_send(p, k, way):
        (owner, half, kind, d) = ways[way]
        blocks = pl.ds(half * DEVB, DEVB)
        return remote(
            part_send[p][k].at[z_to(owner), blocks],
            part_recv[p][k].at[kind, blocks],
            p_s.at[p, k, way],
            p_r.at[p, k, way],
            z_peer(d),
        )

    def local_out(k):
        return pltpu.make_async_copy(
            stage.at[k, 0], out.at[pl.ds(row0 + k * M, M), :], o_l.at[k]
        )

    def sibling_out(k):
        return remote(
            stage.at[k, 1],
            out.at[pl.ds(row0 + k * M, M), :],
            o_s.at[k],
            o_r.at[k],
            sibling,
        )

    barrier = pltpu.get_barrier_semaphore()
    for peer in peers:
        pl.semaphore_signal(barrier, inc=1, device_id=peer, device_id_type=MESH)
    for p in range(2):
        local_ints(p).start()
    for k in range(CHUNKS):
        mine = pl.ds(pl.multiple_of(row0 + k * M, M), M)
        theirs = pl.ds(pl.multiple_of((1 - h) * ROWS + k * M, M), M)
        for b in range(DEVB):
            columns = slice(b * BS, (b + 1) * BS)
            win[0][k][HERE + h * DEVB + b] = amps[mine, columns]
            other_amps[k, b] = amps[theirs, columns]
    pl.semaphore_wait(barrier, len(peers))

    for k in range(CHUNKS):
        sibling_amps(k).start()

    def spread_row(p, k):
        if p == 0:
            sibling_amps(k).wait_recv()
        for d in (1, 3, 2):
            x_send(p, k, d).start()

    def spread_rows(p, k):
        for d in (1, 2, 3):
            x_send(p, k, d).wait_recv()
        y_each(p, k, lambda copy: copy.start())

    def exchange(p, k):
        y_each(p, k, lambda copy: copy.wait_recv())
        source = win[p][k]

        def piece(first, plane):
            start = jnp.clip(first - window_at, 0, WIN - NZ * SLOTS)
            return source[pl.ds(start + plane * SLOTS, SLOTS)]

        for d in (1, 3, 2):
            packed[p][k][d - 1, 0:SLOTS] = piece(head, z_to(d))
            packed[p][k][d - 1, SLOTS : 2 * SLOTS] = piece(tail, z_to(d))
            z_send(p, k, d).start()
        rows = pl.ds(pl.multiple_of(r * M, M), M)
        if inner:
            between = source[pl.ds(jnp.clip(inner_at - window_at, 0, WIN - inner), inner)]
            packed_in[p][k][...] = between
            for d in (1, 2, 3):

                @pl.when(z_to(d) < planes)
                def _():
                    zi_send(p, k, d).start()

            gathered[p][k][2 * SLOTS : 2 * SLOTS + inner, rows] = between
        gathered[p][k][0:SLOTS, rows] = piece(head, r)
        gathered[p][k][SLOTS : 2 * SLOTS, rows] = piece(tail, r)

    def multiply(p, k):
        for d in (1, 2, 3):
            z_send(p, k, d).wait_recv()
        if inner:

            @pl.when(r < planes)
            def _():
                for d in (1, 2, 3):
                    zi_send(p, k, d).wait_recv()

        @pl.loop(0, CHIPB)
        def _(q):
            first, count = group(c * CHIPB + q)
            base = jnp.where(first == head, 0, SLOTS)
            if inner:
                between = (first != head) & (first != tail)
                some = count > r * SLOTS
                place = 2 * SLOTS + first + r * SLOTS - inner_at
                base = jnp.where(between, jnp.where(some, place, 0), base)
                base = jnp.clip(base, 0, 2 * SLOTS + inner - 1)
            tiles = gathered[p][k][pl.ds(base, SLOTS)]
            rows = jnp.concatenate([tiles[i] for i in range(SLOTS)], axis=1)
            product = jnp.dot(rows, ints[p][q], preferred_element_type=jnp.float32)
            product = product.reshape(NZ, M, BS)
            part[k][:, q] = product
            part_send[p][k][:, q] = product.astype(jnp.bfloat16)

        for way in range(4):
            p_send(p, k, way).start()

    def relay(p, k):
        for half in range(2):
            p_send(p, k, half).wait_recv()
            blocks = slice(half * DEVB, (half + 1) * DEVB)
            owner = z_to((1, 3)[half])
            both = part[k][owner, blocks] + part_recv[p][k][2, blocks].astype(jnp.float32)
            part_send[p][k][owner, blocks] = both.astype(jnp.bfloat16)
            p_send(p, k, 4 + half).start()

    def finish(p, k):
        for way in range(2, 6):
            p_send(p, k, way).wait_recv()

        own = pl.ds(pl.multiple_of(row0 + k * M, M), M)

        @pl.loop(0, DEVB)
        def _(b):
            for side in range(2):
                q = (h if side == 0 else 1 - h) * DEVB + b
                total = part[k][r, q]
                for d in range(2):
                    total += part_recv[p][k][d, q].astype(jnp.float32)
                denom = virs[q] - occ[own, :]
                value = win[p][k][HERE + q].astype(jnp.float32) + total / denom
                if p == 0:
                    win[1][k][HERE + q] = value.astype(jnp.bfloat16)
                else:
                    stage[k, side, :, pl.ds(pl.multiple_of(b * BS, BS), BS)] = value

        if p == 1:
            sibling_out(k).start()
            local_out(k).start()

    def mask(p):
        local_ints(p).wait()
        sibling_ints(p).wait_recv()
        slot = lax.broadcasted_iota(jnp.int32, (KW, BS), 0)

        @pl.loop(0, CHIPB)
        def _(q):
            _, count = group(c * CHIPB + q)
            limit = (count - r * SLOTS) * BS
            tile = ints[p][q]
            ints[p][q] = jnp.where(slot < limit, tile, jnp.zeros_like(tile))

    for b in range(DEVB):
        virs[h * DEVB + b] = vir[b]
    if inner:
        for p in range(2):
            for k in range(CHUNKS):
                for b in range(2 * SLOTS + inner, 3 * SLOTS + inner - 1):
                    gathered[p][k][b] = jnp.zeros((NZ * M, BS), jnp.bfloat16)

    masked = set()
    steps = (spread_row, spread_rows, exchange, multiply, relay, finish)

    def do(step, k):
        if step % 6 == 3 and step not in masked:
            masked.add(step)
            mask(step // 6)
            if step == 3:
                sibling_vir().wait_recv()
        steps[step % 6](step // 6, k)
        if (step, k) == (0, 1):
            sibling_vir().start()
            sibling_ints(0).start()
        if (step, k) == (2, 1):
            sibling_ints(1).start()

    for step, k in ORDER:
        do(step, k)

    for p in range(2):
        sibling_ints(p).wait_send()
        for k in range(CHUNKS):
            for d in (1, 2, 3):
                x_send(p, k, d).wait_send()
                z_send(p, k, d).wait_send()
                if inner:

                    @pl.when(z_to(d) < planes)
                    def _():
                        zi_send(p, k, d).wait_send()

            for way in range(6):
                p_send(p, k, way).wait_send()
            y_each(p, k, lambda copy: copy.wait_send())
    sibling_vir().wait_send()
    for k in range(CHUNKS):
        sibling_amps(k).wait_send()
        local_out(k).wait()
        sibling_out(k).wait()


def call(number, operands):
    inner = LEVELS[number][0]
    bf16, f32 = jnp.bfloat16, jnp.float32
    width = 2 * SLOTS + (inner + SLOTS - 1 if inner else 0)
    vmem = pltpu.VMEM
    dma = pltpu.SemaphoreType.DMA
    each = []
    each += [vmem((WIN, M, BS), bf16)] * (2 * CHUNKS)
    each += [vmem((width, NZ * M, BS), bf16)] * (2 * CHUNKS)
    each += [vmem((3, 2 * SLOTS, M, BS), bf16)] * (2 * CHUNKS)
    if inner:
        each += [vmem((inner, M, BS), bf16)] * (2 * CHUNKS)
    each += [vmem((CHIPB, KW, BS), bf16)] * 2
    each += [vmem((NZ, CHIPB, M, BS), f32)] * CHUNKS
    each += [vmem((NZ, CHIPB, M, BS), bf16)] * (2 * CHUNKS)
    each += [vmem((3, CHIPB, M, BS), bf16)] * (2 * CHUNKS)
    each += [vmem((CHIPB, 1, BS), f32), vmem((CHUNKS, 2, M, DW), f32)]
    each += [vmem((CHUNKS, DEVB, M, BS), bf16)]
    three, six = (2, CHUNKS, 3), (2, CHUNKS, 6)
    each += [dma(s) for s in (three, three, six, six, three, three, three, three, six, six)]
    each += [dma((2,))] * 3 + [dma((CHUNKS,))] * 2 + [dma(())] * 2 + [dma((CHUNKS,))] * 3
    hbm = pl.BlockSpec(memory_space=pl.ANY)
    return pl.pallas_call(
        functools.partial(kernel, LEVELS[number]),
        name="ladders",
        out_shape=jax.ShapeDtypeStruct((2 * ROWS, DW), f32),
        in_specs=[
            pl.BlockSpec(memory_space=pltpu.SMEM),
            pl.BlockSpec(memory_space=pltpu.VMEM),
            hbm,
            hbm,
            pl.BlockSpec(memory_space=pltpu.VMEM),
            pl.BlockSpec(memory_space=pltpu.VMEM),
        ],
        out_specs=hbm,
        scratch_shapes=each,
        compiler_params=pltpu.CompilerParams(
            collective_id=1 + number, has_side_effects=True, vmem_limit_bytes=60 << 20
        ),
    )(*operands)


def shards(amps, ladder_ints, cycle_ints, sym_sizes, occ_energy, vir_energy):
    operands = (
        sym_sizes,
        amps,
        ladder_ints.reshape(DEVB, KW, BS),
        cycle_ints.reshape(DEVB, KW, BS),
        occ_energy[:, None],
        vir_energy.reshape(DEVB, 1, BS),
    )
    index = jnp.arange(sym_sizes.shape[0])
    upto = index[None, :] <= index[:, None]
    ends = jnp.sum(jnp.where(upto, sym_sizes[None, :], 0), axis=1)
    starts = ends - sym_sizes
    chip = starts // CHIPB
    inside = (chip == ends // CHIPB) & (starts % CHIPB != 0)
    together = inside[None, :] & (chip[None, :] == chip[:, None])
    most = jnp.max(jnp.sum(jnp.where(together, sym_sizes[None, :], 0), axis=1))
    level = sum((most > inner).astype(jnp.int32) for inner, _ in LEVELS[:-1])
    branches = [functools.partial(call, number) for number in range(len(LEVELS))]
    return lax.switch(level, branches, operands)


def solution(mesh):
    placed = (
        P("red", "ten"),
        P("ten", "red", None, None),
        P("ten", "red", None, None),
        P(),
        P("red"),
        P("ten"),
    )
    return jax.shard_map(
        shards, mesh=mesh, in_specs=placed, out_specs=P("red", "ten"), check_vma=False
    )
```
